512 devices in a mesh: cells: 64 (over x, z), genes: 8 (over y, core).
Axes of the slice: x: 4, y: 4, z: 16, core: 2. Of those that a mesh axis runs over, the one named last changes fastest.
Arguments:
- expression: bfloat16 [262144, 4096], P('cells', 'genes'), may hold values from 0 to 3
- loading: bfloat16 [4096, 128], P('genes'), may hold values from -0.09375 to 0.09375
- kernel_width: bfloat16 [262144], P(('cells', 'genes')), may hold values from 10 to 20
- cluster: int32 [262144, 1], P(('cells', 'genes')), may hold values from 0 to 511, as said below
- quality: int32 [262144], P(('cells', 'genes')), may hold values from 0 to 1, as said below
Outputs:
- smoothed: float32 [262144, 128], P(('cells', 'genes'))
The draws below stay inside these ranges and needn't reach their ends.
Inputs may be any that keep to these rules, and one draw needn't show every extreme that they name: Among the 512 cells of one device no cluster appears more than 2 times; one cluster appears exactly 2 times in every device, so that it holds 1024 cells; every cluster appears somewhere. All cells of a cluster that holds 1024 cells have quality 1.
All inputs are finite; a program needn't handle non-finite values.
Results may differ from the reference program's by a relative error of at most 0.0029.
Values may be sent and summed in bfloat16 or wider, within the bound.
A program may use at most 64 MiB of HBM per device.

```python
import math
import jax
import jax.numpy as jnp
from jax import lax

G = 4096
K = 128
ROWS_DEV = 512
CAP = 2
SLOTS = 1024
CLUSTERS = 512
CELLS = 262144
DEVICES = 512


def labels_and_hot(key):
    hot = jax.random.randint(jax.random.fold_in(key, 1), (), 0, CLUSTERS).astype(jnp.int32)
    others = jax.random.permutation(jax.random.fold_in(key, 2), CLUSTERS - 1).astype(jnp.int32)
    row_ids = jnp.arange(ROWS_DEV, dtype=jnp.int32)
    device_ids = jnp.arange(DEVICES, dtype=jnp.int32)
    ranked = device_ids[:, None] * (ROWS_DEV - CAP) + jnp.maximum(row_ids[None, :] - CAP, 0)
    picked = others[ranked % (CLUSTERS - 1)]
    other_ids = picked + (picked >= hot).astype(jnp.int32)
    base = jnp.where(row_ids[None, :] < CAP, hot, other_ids).astype(jnp.int32)
    device_keys = jax.random.split(jax.random.fold_in(key, 3), DEVICES)
    orders = jax.vmap(lambda one_key: jax.random.permutation(one_key, ROWS_DEV))(device_keys).astype(jnp.int32)
    labels = jnp.take_along_axis(base, orders, axis=1).reshape(DEVICES * ROWS_DEV).astype(jnp.int32)
    return (labels, hot)


def draw_cluster(key, part):
    labels, hot = labels_and_hot(key)
    return labels[:, None].astype(jnp.int32)


def draw_quality(key, part):
    labels, hot = labels_and_hot(key)
    rolls = jax.random.randint(jax.random.fold_in(key, 7), (DEVICES * ROWS_DEV,), 0, 5)
    passed = (rolls < 4) | (labels == hot)
    return passed.astype(jnp.int32)


def level_of(key, extent, cuts, least, high):
    loudness = 1.0
    for axis_at, parts in cuts:
        draws = jax.random.uniform(jax.random.fold_in(jax.random.fold_in(key, 6), axis_at), (parts,), jnp.float32, least / len(cuts), high / len(cuts))
        loudness = loudness * jnp.repeat(jnp.exp(draws), extent[axis_at] // parts).reshape((-1,) + (1,) * (len(extent) - 1 - axis_at))
    return loudness


def scatter_about(own_key, dims, deviation, limit, pieces=(), kind=jnp.bfloat16):
    drawn = jax.random.normal(own_key, dims, jnp.float32) * deviation
    if len(pieces) > 0:
        drawn = level_of(own_key, dims, pieces, -0.22, 0.18) * drawn
    return jnp.clip(drawn, min=-limit, max=limit).astype(kind)


def setup_inputs(seed: int = 0) -> dict:
    key_list = jax.random.split(jax.random.key(seed), 6)
    expression = jnp.clip(3.0 * jax.random.uniform(key_list[0], (CELLS, G), jnp.float32) ** level_of(key_list[0], (CELLS, G), ((0, 64), (1, 8)), -0.2, 0.2), 0.0, 3.0).astype(jnp.bfloat16)
    loading = scatter_about(key_list[1], (G, K), G ** -0.5, 0.09375, ((0, 8),))
    kernel_width = jnp.clip(jnp.exp(math.log(20.0) - 0.6931472 * jax.random.uniform(key_list[2], (CELLS,), jnp.float32) ** level_of(key_list[2], (CELLS,), ((0, 512),), -0.2, 0.2)), 10.0, 20.0).astype(jnp.bfloat16)
    cluster = draw_cluster(jax.random.fold_in(key_list[5], 71), 0)
    quality = draw_quality(jax.random.fold_in(key_list[5], 71), 0)
    return dict(expression=expression, loading=loading, kernel_width=kernel_width, cluster=cluster, quality=quality)


def diffuse(slot_rows, widths):
    widths = widths.astype(jnp.float32)
    present = (widths > 0).astype(jnp.float32)
    as_float = slot_rows.astype(jnp.float32)
    sq_norms = jnp.sum(as_float * as_float, axis=1)
    products = jnp.dot(slot_rows, slot_rows.T, preferred_element_type=jnp.float32)
    distance = sq_norms[:, None] + sq_norms[None, :] - 2.0 * products
    pair_live = present[:, None] * present[None, :]
    width_pair = jnp.where(pair_live > 0, widths[:, None] * widths[None, :], jnp.ones_like(pair_live))
    affinity = jnp.exp(-distance / width_pair) * pair_live
    row_total = jnp.sum(affinity, axis=1) + (1.0 - present)
    weights = (affinity / row_total[:, None]).astype(jnp.bfloat16)
    one_step = 0.5 * (as_float + jnp.dot(weights, slot_rows, preferred_element_type=jnp.float32))
    two_steps = 0.5 * (one_step + jnp.dot(weights, one_step.astype(jnp.bfloat16), preferred_element_type=jnp.float32))
    return two_steps


def reference(expression, loading, kernel_width, cluster, quality):
    embedded = jnp.dot(expression, loading, preferred_element_type=jnp.float32).astype(jnp.bfloat16)
    labels = cluster[:, 0].astype(jnp.int32)
    is_live = quality == 1
    keyed_ids = jnp.where(is_live, labels, CLUSTERS).astype(jnp.int32)
    sort_order = jnp.argsort(keyed_ids, stable=True).astype(jnp.int32)
    counts = jax.ops.segment_sum(jnp.ones_like(keyed_ids), keyed_ids, num_segments=CLUSTERS + 1).astype(jnp.int32)
    starts = (jnp.cumsum(counts) - counts).astype(jnp.int32)
    padded_rows = jnp.concatenate([embedded[sort_order], jnp.zeros((SLOTS, K), embedded.dtype)], 0)
    padded_band = jnp.concatenate([kernel_width[sort_order], jnp.zeros((SLOTS,), kernel_width.dtype)], 0)

    def one_cluster(cluster_index):
        block_start = starts[cluster_index].astype(jnp.int32)
        rows_block = lax.dynamic_slice_in_dim(padded_rows, block_start, SLOTS, 0)
        band_block = lax.dynamic_slice_in_dim(padded_band, block_start, SLOTS, 0)
        present = jnp.arange(SLOTS, dtype=jnp.int32) < counts[cluster_index]
        band_block = jnp.where(present, band_block, jnp.zeros_like(band_block))
        return diffuse(rows_block, band_block)

    blocks = lax.map(one_cluster, jnp.arange(CLUSTERS, dtype=jnp.int32))
    position = jnp.argsort(sort_order).astype(jnp.int32)
    safe_ids = jnp.minimum(keyed_ids, CLUSTERS - 1).astype(jnp.int32)
    flat_index = jnp.clip(safe_ids * SLOTS + position - starts[safe_ids], 0, CLUSTERS * SLOTS - 1).astype(jnp.int32)
    gathered = blocks.reshape(CLUSTERS * SLOTS, K)[flat_index]
    return jnp.where(is_live[:, None], gathered, embedded.astype(jnp.float32))
```

```python
import functools

import jax
import jax.numpy as jnp
from jax import lax
from jax.experimental import pallas as pl
from jax.experimental.pallas import tpu as pltpu
from jax.sharding import PartitionSpec as P

MESH = pl.DeviceIdType.MESH
F32 = jnp.float32
BF16 = jnp.bfloat16
I32 = jnp.int32

X, Z, Y = 4, 16, 4
GROUP = 8
ROWS = 512
HALF = ROWS // 2
COMPS = 128
SLOTS = 1024
CHUNK = 256
PIECE = 32
TILE = 16
DY_ORDER = (2, 1, 3, 0)
DX_ORDER = (2, 1, 3, 0)


def iota(shape, dim):
    return lax.broadcasted_iota(I32, shape, dim)


def dot(a, b):
    return jnp.dot(a, b, preferred_element_type=F32)


def dot_nt(a, b):
    return lax.dot_general(a, b, (((1,), (1,)), ((), ())), preferred_element_type=F32)


def as_columns(row):
    n = row.shape[1]
    return jnp.concatenate(
        [jnp.broadcast_to(row[:, m : m + 128], (128, 128)).T for m in range(0, n, 128)], axis=0
    )


def as_row(columns):
    n = columns.shape[0]
    return jnp.concatenate([columns[m : m + 128, :].T[0:1, :] for m in range(0, n, 128)], axis=1)


def far_first(t):
    return 8 + (1 - 2 * (t % 2)) * ((t + 1) // 2)


def kernel(
    expr, load_ref, width_ref, cluster_ref, quality_ref, out_ref,
    xbuf, sib_out, sib_in, a_out, a_in, b_out, b_in, s_keep, e_keep,
    hot, hot_t, p1, r1, p2, emb, w1, w1_in, w2, w2_in, rw_col, rw_row,
    aff, o_keep, s1_ref, p3, r3, p4, r4,
    x_sem, sib_s, sib_r, a_s, a_r, b_s, b_r, s1_s, s1_r, s2_s, s2_r, s3_s, s3_r, s4_s, s4_r,
    w1_s, w1_r, w2_s, w2_r,
):
    q = lax.axis_index("cells")
    g = lax.axis_index("genes")
    x, z = q // Z, q % Z
    y, core = g // 2, g % 2
    other = 1 - core

    def remote(src, dst, ssem, rsem, dev):
        return pltpu.make_async_remote_copy(
            src_ref=src, dst_ref=dst, send_sem=ssem, recv_sem=rsem,
            device_id=dev, device_id_type=MESH,
        )

    def at_y(dy):
        return (q, ((y + dy) % Y) * 2 + core)

    sibling = (q, y * 2 + other)

    def fetch(i):
        dy, c = DY_ORDER[i % 4], (other if i < 4 else core)
        block = ((y + dy) % Y) * 2 + c
        return pltpu.make_async_copy(
            expr.at[pl.ds(pl.multiple_of(block * ROWS, ROWS), ROWS)], xbuf.at[i], x_sem.at[i]
        )

    for i in range(8):
        fetch(i).start()

    barrier = pltpu.get_barrier_semaphore()

    @pl.loop(1, GROUP)
    def _(d):
        pl.semaphore_signal(barrier, 1, device_id=(q, (g + d) % GROUP), device_id_type=MESH)

    @pl.loop(1, X * Z)
    def _(j):
        dev = (((x + j // Z) % X) * Z + (z + j % Z) % Z, g)
        pl.semaphore_signal(barrier, 1, device_id=dev, device_id_type=MESH)

    loading = load_ref[...]
    for i in range(4):
        fetch(i).wait()
        sib_out[i] = dot(xbuf[i], loading)
        if i == 0:
            pl.semaphore_wait(barrier, GROUP - 1 + X * Z - 1)
        remote(sib_out.at[i], sib_in.at[i], sib_s.at[i], sib_r.at[i], sibling).start()

    def chip_sum(i):
        fetch(4 + i).wait()
        part = dot(xbuf[4 + i], loading)
        remote(sib_out.at[i], sib_in.at[i], sib_s.at[i], sib_r.at[i], sibling).wait_recv()
        return part + sib_in[i]

    up, down = at_y(1), at_y(3)
    low, high = pl.ds(0, HALF), pl.ds(HALF, HALF)
    a_out[...] = chip_sum(0).astype(BF16)
    a_up = remote(a_out.at[low], a_in.at[0], a_s.at[0], a_r.at[0], up)
    a_down = remote(a_out.at[high], a_in.at[1], a_s.at[1], a_r.at[1], down)
    a_up.start()
    a_down.start()
    part = chip_sum(1)
    b_out[0, HALF:, :] = part[HALF:].astype(BF16)
    b_up_high = remote(b_out.at[0, high], b_in.at[0, high], b_s.at[0], b_r.at[0], up)
    b_up_high.start()
    s_keep[0] = part[:HALF]
    part = chip_sum(2)
    b_out[1, :HALF, :] = part[:HALF].astype(BF16)
    b_down_low = remote(b_out.at[1, low], b_in.at[1, low], b_s.at[1], b_r.at[1], down)
    b_down_low.start()
    s_keep[1] = part[HALF:]
    e_keep[...] = chip_sum(3)

    cluster = cluster_ref[...]
    live = quality_ref[...] == 1
    owner = cluster % (X * Z)
    gd = cluster // (X * Z)
    dx = (owner // Z - x + X) % X
    dz = (owner % Z - z + Z) % Z
    key = jnp.where(live, cluster, -1).astype(F32)
    key_col = as_columns(key)
    ranks = []
    for m in range(4):
        row = key[:, m * 128 : m * 128 + 128]
        same = (key_col[m * 128 : m * 128 + 128] == row) & (
            iota((128, 128), 0) < iota((128, 128), 1)
        )
        rank = jnp.sum(same.astype(F32), axis=0, keepdims=True)
        for k in range(m):
            same = key_col[k * 128 : k * 128 + 128] == row
            rank += jnp.sum(same.astype(F32), axis=0, keepdims=True)
        ranks.append(rank)
    rank = jnp.concatenate(ranks, axis=1).astype(I32)
    slot = jnp.where(live, dx * CHUNK + gd * PIECE + dz * 2 + rank, -1)
    place = jnp.where(live, dx * PIECE + dz * 2 + rank, -1)
    width = width_ref[...].astype(F32)
    m1 = jnp.where((iota((16, ROWS), 0) == gd) & live, width, 0.0).astype(BF16)
    m2 = (as_columns(place.astype(F32)).astype(I32) == iota((ROWS, 128), 1)).astype(F32).astype(BF16)
    w1_all = dot(m1, m2)
    for k in range(GROUP):
        w1[k] = w1_all[k : k + 1]
    w1_in[g] = w1[g]

    @pl.loop(1, GROUP)
    def _(d):
        to = (g + d) % GROUP
        remote(w1.at[to], w1_in.at[g], w1_s, w1_r, (q, to)).start()

    a_up.wait_recv()
    b_out[0, :HALF, :] = (s_keep[0] + a_in[0].astype(F32)).astype(BF16)
    b_up_low = remote(b_out.at[0, low], b_in.at[0, low], b_s.at[2], b_r.at[2], up)
    b_up_low.start()
    a_down.wait_recv()
    b_out[1, HALF:, :] = (s_keep[1] + a_in[1].astype(F32)).astype(BF16)
    b_down_high = remote(b_out.at[1, high], b_in.at[1, high], b_s.at[3], b_r.at[3], down)
    b_down_high.start()

    for m in range(4):
        hot[m * CHUNK : (m + 1) * CHUNK, :] = (
            (iota((CHUNK, ROWS), 0) + m * CHUNK == slot).astype(F32).astype(BF16)
        )
    slot_col = as_columns(slot.astype(F32)).astype(I32)
    for m in range(8):
        hot_t[:, m * 128 : (m + 1) * 128] = (
            (slot_col == iota((ROWS, 128), 1) + m * 128).astype(F32).astype(BF16)
        )
    o, i = iota((CHUNK, CHUNK), 0), iota((CHUNK, CHUNK), 1)
    perm = (((o // 2) % 8) * PIECE + (o // TILE) * 2 + o % 2 == i).astype(F32).astype(BF16)
    perm_t = (((i // 2) % 8) * PIECE + (i // TILE) * 2 + i % 2 == o).astype(F32).astype(BF16)

    remote(w1.at[pl.ds(0, 7)], w1_in.at[pl.ds(0, 7)], w1_s, w1_r, sibling).wait_recv()
    w1_rows = jnp.concatenate(
        [w1_in[k] for k in range(GROUP)] + [jnp.zeros((120, 128), F32)], axis=0
    ).astype(BF16)
    w2_all = jnp.zeros((64, 128), F32)
    for r in range(2):
        pick = (iota((64, 128), 0) * 2 + r == iota((64, 128), 1)).astype(F32).astype(BF16)
        put = (iota((128, 128), 0) * 2 + r == iota((128, 128), 1)).astype(F32).astype(BF16)
        w2_all += dot(dot_nt(pick, w1_rows).astype(BF16), put)
    for k in range(64):
        w2[k] = w2_all[k : k + 1]
    w2_in[0] = w2[0]

    b_up_high.wait_recv()
    b_down_low.wait_recv()
    b_up_low.wait_recv()
    b_down_high.wait_recv()
    embedded = e_keep[...] + b_in[0].astype(F32) + b_in[1].astype(F32)
    e_keep[...] = embedded
    e_rows = embedded.astype(BF16)

    for k in DX_ORDER:
        p1[k] = dot(hot[k * CHUNK : (k + 1) * CHUNK, :], e_rows).astype(BF16)

        @pl.loop(1, GROUP)
        def _(d):
            to = (g + d) % GROUP
            remote(
                p1.at[k, pl.ds(pl.multiple_of(to * PIECE, PIECE), PIECE)],
                r1.at[k, pl.ds(pl.multiple_of(g * PIECE, PIECE), PIECE)],
                s1_s.at[k], s1_r.at[k], (q, to),
            ).start()

        mine = pl.ds(pl.multiple_of(g * PIECE, PIECE), PIECE)
        r1[k, mine, :] = p1[k, mine, :]

    @pl.loop(1, X * Z)
    def _(j):
        dev = (((x + j // Z) % X) * Z + (z + j % Z) % Z, g)
        remote(w2.at[j], w2_in.at[j], w2_s, w2_r, dev).start()

    def all_but_one(src, dst, ssem, rsem):
        n = CHUNK - PIECE
        return remote(src.at[pl.ds(0, n)], dst.at[pl.ds(0, n)], ssem, rsem, sibling)

    def tiles(k, src, dst, ssem, rsem):
        n = CHUNK - TILE if k == 0 else CHUNK
        return remote(src.at[pl.ds(0, n)], dst.at[pl.ds(0, n)], ssem, rsem, sibling)

    for k in DX_ORDER:
        all_but_one(p1.at[k], r1.at[k], s1_s.at[k], s1_r.at[k]).wait_recv()
        p2[k] = dot(perm, r1[k]).astype(BF16)

        @pl.loop(0, Z - 1 if k == 0 else Z)
        def _(t):
            d = far_first(t)
            rows = pl.ds(pl.multiple_of(d * TILE, TILE), TILE)
            dev = (((x + k) % X) * Z + (z + d) % Z, g)
            remote(p2.at[k, rows], emb.at[k, rows], s2_s.at[k], s2_r.at[k], dev).start()

        if k == 0:
            emb[0, :TILE, :] = p2[0, :TILE, :]

    remote(w2.at[pl.ds(0, 63)], w2_in.at[pl.ds(0, 63)], w2_s, w2_r, sibling).wait_recv()
    w2_rows = jnp.concatenate(
        [w2_in[k] for k in range(64)] + [jnp.zeros((64, 128), F32)], axis=0
    ).astype(BF16)
    s, lane = iota((SLOTS, 128), 0), iota((SLOTS, 128), 1)
    spread = dot((s // TILE == lane).astype(F32).astype(BF16), w2_rows)
    own = jnp.where(s % TILE == lane, spread, 0.0).astype(BF16)
    w_col = dot(own, jnp.ones((128, 128), BF16))
    rw = jnp.where(w_col > 0, 1.0 / jnp.where(w_col > 0, w_col, 1.0), 0.0)
    rw_col[...] = rw
    rw_row[...] = as_row(rw)

    for k in DX_ORDER:
        tiles(k, p2.at[k], emb.at[k], s2_s.at[k], s2_r.at[k]).wait_recv()

    rows = emb[...].reshape(SLOTS, COMPS)
    wide = rows.astype(F32)
    norm = jnp.broadcast_to(jnp.sum(wide * wide, axis=1, keepdims=True), (SLOTS, 128))
    norm_row = as_row(norm)
    present = (rw_col[...] > 0).astype(F32).astype(BF16)
    with_ones = jnp.concatenate([rows, present], axis=1)
    for k in range(4):
        part = slice(k * CHUNK, (k + 1) * CHUNK)
        products = dot_nt(rows[part], rows)
        distance = norm[part, 0:1] + norm_row - 2.0 * products
        affinity = jnp.exp(-distance * rw_col[part, 0:1] * rw_row[...]).astype(BF16)
        aff[k] = affinity
        both = dot(affinity, with_ones)
        here = rw_col[part, :] > 0
        inverse = jnp.where(here, 1.0 / jnp.where(here, both[:, COMPS:], 1.0), 0.0)
        moved = both[:, :COMPS] * inverse
        o_keep[k] = 0.25 * moved
        rw_col[part, :] = 0.5 * inverse
        s1_ref[part, :] = jnp.where(here, 0.5 * (wide[part] + moved), 0.0).astype(BF16)

    for k in DX_ORDER:
        part = slice(k * CHUNK, (k + 1) * CHUNK)
        p3[k] = (o_keep[k] + rw_col[part, :] * dot(aff[k], s1_ref[...])).astype(BF16)

        @pl.loop(0, Z - 1 if k == 0 else Z)
        def _(t):
            d = far_first(t)
            rows = pl.ds(pl.multiple_of(d * TILE, TILE), TILE)
            dev = (((x - k + X) % X) * Z + (z - d + Z) % Z, g)
            remote(p3.at[k, rows], r3.at[k, rows], s3_s.at[k], s3_r.at[k], dev).start()

        if k == 0:
            r3[0, :TILE, :] = p3[0, :TILE, :]

    for k in DX_ORDER:
        tiles(k, p3.at[k], r3.at[k], s3_s.at[k], s3_r.at[k]).wait_recv()
        p4[k] = dot(perm_t, r3[k]).astype(BF16)

        @pl.loop(1, GROUP)
        def _(d):
            to = (g + d) % GROUP
            remote(
                p4.at[k, pl.ds(pl.multiple_of(to * PIECE, PIECE), PIECE)],
                r4.at[k, pl.ds(pl.multiple_of(g * PIECE, PIECE), PIECE)],
                s4_s.at[k], s4_r.at[k], (q, to),
            ).start()

        mine = pl.ds(pl.multiple_of(g * PIECE, PIECE), PIECE)
        r4[k, mine, :] = p4[k, mine, :]

    live_col = as_columns(quality_ref[...].astype(F32)) == 1.0
    total = jnp.where(live_col, 0.25, 1.0) * e_keep[...]
    for k in DX_ORDER:
        all_but_one(p4.at[k], r4.at[k], s4_s.at[k], s4_r.at[k]).wait_recv()
        total += dot(hot_t[:, k * CHUNK : (k + 1) * CHUNK], r4[k])
    out_ref[...] = total

    for i in range(4):
        remote(sib_out.at[i], sib_in.at[i], sib_s.at[i], sib_r.at[i], sibling).wait_send()
    for copy in (a_up, a_down, b_up_high, b_down_low, b_up_low, b_down_high):
        copy.wait_send()
    remote(w1.at[pl.ds(0, 7)], w1_in.at[pl.ds(0, 7)], w1_s, w1_r, sibling).wait_send()
    remote(w2.at[pl.ds(0, 63)], w2_in.at[pl.ds(0, 63)], w2_s, w2_r, sibling).wait_send()
    for k in DX_ORDER:
        all_but_one(p1.at[k], r1.at[k], s1_s.at[k], s1_r.at[k]).wait_send()
        tiles(k, p2.at[k], emb.at[k], s2_s.at[k], s2_r.at[k]).wait_send()
        tiles(k, p3.at[k], r3.at[k], s3_s.at[k], s3_r.at[k]).wait_send()
        all_but_one(p4.at[k], r4.at[k], s4_s.at[k], s4_r.at[k]).wait_send()


def body(expression, loading, kernel_width, cluster, quality):
    vmem = pl.BlockSpec(memory_space=pltpu.VMEM)
    dma = pltpu.SemaphoreType.DMA
    chunks = pltpu.VMEM((4, CHUNK, COMPS), BF16)
    return pl.pallas_call(
        kernel,
        out_shape=jax.ShapeDtypeStruct((ROWS, COMPS), F32),
        in_specs=[pl.BlockSpec(memory_space=pl.ANY), vmem, vmem, vmem, vmem],
        out_specs=vmem,
        scratch_shapes=[
            pltpu.VMEM((8, ROWS, 512), BF16),
            pltpu.VMEM((4, ROWS, COMPS), F32),
            pltpu.VMEM((4, ROWS, COMPS), F32),
            pltpu.VMEM((ROWS, COMPS), BF16),
            pltpu.VMEM((2, HALF, COMPS), BF16),
            pltpu.VMEM((2, ROWS, COMPS), BF16),
            pltpu.VMEM((2, ROWS, COMPS), BF16),
            pltpu.VMEM((2, HALF, COMPS), F32),
            pltpu.VMEM((ROWS, COMPS), F32),
            pltpu.VMEM((SLOTS, ROWS), BF16),
            pltpu.VMEM((ROWS, SLOTS), BF16),
            chunks,
            chunks,
            chunks,
            chunks,
            pltpu.VMEM((GROUP, 1, 128), F32),
            pltpu.VMEM((GROUP, 1, 128), F32),
            pltpu.VMEM((X * Z, 1, 128), F32),
            pltpu.VMEM((X * Z, 1, 128), F32),
            pltpu.VMEM((SLOTS, 128), F32),
            pltpu.VMEM((1, SLOTS), F32),
            pltpu.VMEM((4, CHUNK, SLOTS), BF16),
            pltpu.VMEM((4, CHUNK, COMPS), F32),
            pltpu.VMEM((SLOTS, COMPS), BF16),
            chunks,
            chunks,
            chunks,
            chunks,
            dma((8,)), dma((4,)), dma((4,)), dma((2,)), dma((2,)), dma((4,)), dma((4,)),
            dma((4,)), dma((4,)), dma((4,)), dma((4,)), dma((4,)), dma((4,)), dma((4,)), dma((4,)),
            dma, dma, dma, dma,
        ],
        compiler_params=pltpu.CompilerParams(
            collective_id=0, has_side_effects=True, vmem_limit_bytes=48 * 1024 * 1024
        ),
    )(
        expression,
        loading,
        kernel_width.reshape(1, ROWS),
        cluster.reshape(1, ROWS),
        quality.reshape(1, ROWS),
    )


def solution(mesh):
    return jax.shard_map(
        body,
        mesh=mesh,
        in_specs=(
            P("cells", "genes"),
            P("genes", None),
            P(("cells", "genes")),
            P(("cells", "genes"), None),
            P(("cells", "genes")),
        ),
        out_specs=P(("cells", "genes"), None),
        check_vma=False,
    )
```

```python
import functools

import jax
import jax.numpy as jnp
from jax import lax
from jax.experimental import pallas as pl
from jax.experimental.pallas import tpu as pltpu
from jax.sharding import PartitionSpec as P

MESH = pl.DeviceIdType.MESH
F32 = jnp.float32
BF16 = jnp.bfloat16
I32 = jnp.int32

X, Z, Y = 4, 16, 4
GROUP = 8
ROWS = 512
HALF = ROWS // 2
COMPS = 128
SLOTS = 1024
CHUNK = 256
PIECE = 32
TILE = 16
DY_ORDER = (2, 1, 3, 0)
DX_ORDER = (2, 1, 3, 0)


def iota(shape, dim):
    return lax.broadcasted_iota(I32, shape, dim)


def dot(a, b):
    return jnp.dot(a, b, preferred_element_type=F32)


def dot_nt(a, b):
    return lax.dot_general(a, b, (((1,), (1,)), ((), ())), preferred_element_type=F32)


def as_columns(row):
    n = row.shape[1]
    return jnp.concatenate(
        [jnp.broadcast_to(row[:, m : m + 128], (128, 128)).T for m in range(0, n, 128)], axis=0
    )


def as_row(columns):
    n = columns.shape[0]
    return jnp.concatenate([columns[m : m + 128, :].T[0:1, :] for m in range(0, n, 128)], axis=1)


def far_first(t):
    return 8 + (1 - 2 * (t % 2)) * ((t + 1) // 2)


def kernel(
    expr, load_hbm, width_hbm, cluster_hbm, quality_hbm, out_ref,
    xbuf, parts, perm_t, load_ref, width_ref, cluster_ref, quality_ref, sib_out, sib_in, a_out, a_in, b_out, b_in, s_keep, e_keep,
    hot, hot_t, p1, r1, p2, emb, w1, w1_in, w2, wx, w2_in, rw_col, rw_row,
    aff, o_keep, s1_ref, p3, r3, p4, r4,
    x_sem, in_sem, sib_s, sib_r, a_s, a_r, b_s, b_r, s1_s, s1_r, s2_s, s2_r, s3_s, s3_r, s4_s, s4_r,
    w1_s, w1_r, wx_s, wx_r, w2_s, w2_r,
):
    q = lax.axis_index("cells")
    g = lax.axis_index("genes")
    x, z = q // Z, q % Z
    y, core = g // 2, g % 2
    other = 1 - core

    def remote(src, dst, ssem, rsem, dev):
        return pltpu.make_async_remote_copy(
            src_ref=src, dst_ref=dst, send_sem=ssem, recv_sem=rsem,
            device_id=dev, device_id_type=MESH,
        )

    def at_y(dy):
        return (q, ((y + dy) % Y) * 2 + core)

    sibling = (q, y * 2 + other)
    sent = []

    def finish():
        for copy in sent:
            copy.wait_send()

    def fetch(i):
        dy, c = DY_ORDER[i % 4], (other if i < 4 else core)
        block = ((y + dy) % Y) * 2 + c
        return pltpu.make_async_copy(
            expr.at[pl.ds(pl.multiple_of(block * ROWS, ROWS), ROWS)], xbuf.at[i], x_sem.at[i]
        )

    small = [
        pltpu.make_async_copy(src, dst, in_sem.at[i])
        for i, (src, dst) in enumerate(
            [
                (load_hbm, load_ref),
                (cluster_hbm, cluster_ref),
                (quality_hbm, quality_ref),
                (width_hbm, width_ref),
            ]
        )
    ]
    small[0].start()
    for i in range(8):
        fetch(i).start()
    for copy in small[1:]:
        copy.start()

    barrier = pltpu.get_barrier_semaphore()

    @pl.loop(0, X * Z - 1)
    def _(j):
        dev = (((x + 1 + j % X) % X) * Z + (z + far_first(j // X)) % Z, g)
        pl.semaphore_signal(barrier, 1, device_id=dev, device_id_type=MESH)

    @pl.loop(1, GROUP)
    def _(d):
        pl.semaphore_signal(barrier, 1, device_id=(q, (g + d) % GROUP), device_id_type=MESH)

    small[0].wait()
    loading = load_ref[...]
    for i in range(4):
        fetch(i).wait()
        sib_out[i] = dot(xbuf[i], loading)
    for i in range(4):
        fetch(4 + i).wait()
        parts[i] = dot(xbuf[4 + i], loading)
    pl.semaphore_wait(barrier, GROUP - 1 + X * Z - 1)
    for i in range(4):
        sent.append(remote(sib_out.at[i], sib_in.at[i], sib_s.at[i], sib_r.at[i], sibling))
        sent[-1].start()

    def chip_sum(i):
        sent[i].wait_recv()
        return parts[i] + sib_in[i]

    up, down = at_y(1), at_y(3)
    low, high = pl.ds(0, HALF), pl.ds(HALF, HALF)
    a_out[...] = chip_sum(0).astype(BF16)
    a_up = remote(a_out.at[low], a_in.at[0], a_s.at[0], a_r.at[0], up)
    a_down = remote(a_out.at[high], a_in.at[1], a_s.at[1], a_r.at[1], down)
    a_up.start()
    sent.append(a_up)
    a_down.start()
    sent.append(a_down)
    part = chip_sum(1)
    b_out[0, HALF:, :] = part[HALF:].astype(BF16)
    b_up_high = remote(b_out.at[0, high], b_in.at[0, high], b_s.at[0], b_r.at[0], up)
    b_up_high.start()
    sent.append(b_up_high)
    s_keep[0] = part[:HALF]
    part = chip_sum(2)
    b_out[1, :HALF, :] = part[:HALF].astype(BF16)
    b_down_low = remote(b_out.at[1, low], b_in.at[1, low], b_s.at[1], b_r.at[1], down)
    b_down_low.start()
    sent.append(b_down_low)
    s_keep[1] = part[HALF:]
    e_keep[...] = chip_sum(3)

    for copy in small[1:]:
        copy.wait()
    cluster = cluster_ref[...]
    live = quality_ref[...] == 1
    owner = cluster % (X * Z)
    gd = cluster // (X * Z)
    dx = (owner // Z - x + X) % X
    dz = (owner % Z - z + Z) % Z
    key = jnp.where(live, cluster, -1).astype(F32)
    key_col = as_columns(key)
    ranks = []
    for m in range(4):
        row = key[:, m * 128 : m * 128 + 128]
        same = (key_col[m * 128 : m * 128 + 128] == row) & (
            iota((128, 128), 0) < iota((128, 128), 1)
        )
        rank = jnp.sum(same.astype(F32), axis=0, keepdims=True)
        for k in range(m):
            same = key_col[k * 128 : k * 128 + 128] == row
            rank += jnp.sum(same.astype(F32), axis=0, keepdims=True)
        ranks.append(rank)
    rank = jnp.concatenate(ranks, axis=1).astype(I32)
    slot = jnp.where(live, dx * CHUNK + gd * PIECE + dz * 2 + rank, -1)
    place = jnp.where(live, dx * PIECE + dz * 2 + rank, -1)
    width = width_ref[...].reshape(1, ROWS).astype(F32)
    m1 = jnp.where((iota((16, ROWS), 0) == gd) & live, width, 0.0).astype(BF16)
    m2 = (as_columns(place.astype(F32)).astype(I32) == iota((ROWS, 128), 1)).astype(F32).astype(BF16)
    w1_all = dot(m1, m2)
    for k in range(GROUP):
        w1[k] = w1_all[k : k + 1]
    w1_in[g] = w1[g]

    @pl.loop(1, GROUP)
    def _(d):
        to = (g + d) % GROUP
        remote(w1.at[to], w1_in.at[g], w1_s, w1_r, (q, to)).start()

    for m in range(4):
        hot[m * CHUNK : (m + 1) * CHUNK, :] = (
            (iota((CHUNK, ROWS), 0) + m * CHUNK == slot).astype(F32).astype(BF16)
        )
    w1_group = remote(w1.at[pl.ds(0, 7)], w1_in.at[pl.ds(0, 7)], w1_s, w1_r, sibling)
    sent.append(w1_group)
    a_up.wait_recv()
    b_out[0, :HALF, :] = (s_keep[0] + a_in[0].astype(F32)).astype(BF16)
    b_up_low = remote(b_out.at[0, low], b_in.at[0, low], b_s.at[2], b_r.at[2], up)
    b_up_low.start()
    sent.append(b_up_low)
    a_down.wait_recv()
    b_out[1, HALF:, :] = (s_keep[1] + a_in[1].astype(F32)).astype(BF16)
    b_down_high = remote(b_out.at[1, high], b_in.at[1, high], b_s.at[3], b_r.at[3], down)
    b_down_high.start()
    sent.append(b_down_high)

    o, i = iota((CHUNK, CHUNK), 0), iota((CHUNK, CHUNK), 1)
    perm = (((o // 2) % 8) * PIECE + (o // TILE) * 2 + o % 2 == i).astype(F32).astype(BF16)

    w1_group.wait_recv()
    w1_rows = jnp.concatenate(
        [w1_in[k] for k in range(GROUP)] + [jnp.zeros((120, 128), F32)], axis=0
    ).astype(BF16)
    w2_all = jnp.zeros((64, 128), F32)
    for r in range(2):
        pick = (iota((64, 128), 0) * 2 + r == iota((64, 128), 1)).astype(F32).astype(BF16)
        put = (iota((128, 128), 0) * 2 + r == iota((128, 128), 1)).astype(F32).astype(BF16)
        w2_all += dot(dot_nt(pick, w1_rows).astype(BF16), put)
    for k in range(64):
        w2[k // Z, k % Z] = w2_all[k : k + 1]
    for k in range(Z):
        wx[0, k] = w2[0, k]
    for k in range(1, X):
        sent.append(
            remote(w2.at[k], wx.at[k], wx_s.at[k], wx_r.at[k], (((x + k) % X) * Z + z, g))
        )
        sent[-1].start()
    wx_copies = sent[-3:]

    b_up_high.wait_recv()
    b_down_low.wait_recv()
    b_up_low.wait_recv()
    b_down_high.wait_recv()
    embedded = e_keep[...] + b_in[0].astype(F32) + b_in[1].astype(F32)
    e_keep[...] = embedded
    e_rows = embedded.astype(BF16)

    for k in DX_ORDER:
        p1[k] = dot(hot[k * CHUNK : (k + 1) * CHUNK, :], e_rows).astype(BF16)

        @pl.loop(1, GROUP)
        def _(d):
            to = (g + d) % GROUP
            remote(
                p1.at[k, pl.ds(pl.multiple_of(to * PIECE, PIECE), PIECE)],
                r1.at[k, pl.ds(pl.multiple_of(g * PIECE, PIECE), PIECE)],
                s1_s.at[k], s1_r.at[k], (q, to),
            ).start()

        mine = pl.ds(pl.multiple_of(g * PIECE, PIECE), PIECE)
        r1[k, mine, :] = p1[k, mine, :]

    for copy in wx_copies:
        copy.wait_recv()
    for k in range(X):
        w2_in[k, 0] = wx[k, 0]

    @pl.loop(0, Z - 1)
    def _(t):
        d = far_first(t)
        remote(wx.at[:, d], w2_in.at[:, d], w2_s, w2_r, (x * Z + (z + d) % Z, g)).start()

    w2_group = remote(wx.at[:, pl.ds(0, Z - 1)], w2_in.at[:, pl.ds(0, Z - 1)], w2_s, w2_r, sibling)
    sent.append(w2_group)

    def all_but_one(src, dst, ssem, rsem):
        n = CHUNK - PIECE
        return remote(src.at[pl.ds(0, n)], dst.at[pl.ds(0, n)], ssem, rsem, sibling)

    def tiles(k, src, dst, ssem, rsem):
        n = CHUNK - TILE if k == 0 else CHUNK
        return remote(src.at[pl.ds(0, n)], dst.at[pl.ds(0, n)], ssem, rsem, sibling)

    for k in DX_ORDER:
        arrived = all_but_one(p1.at[k], r1.at[k], s1_s.at[k], s1_r.at[k])
        arrived.wait_recv()
        sent.append(arrived)
        p2[k] = dot(perm, r1[k]).astype(BF16)

        @pl.loop(0, Z - 1 if k == 0 else Z)
        def _(t):
            d = far_first(t)
            rows = pl.ds(pl.multiple_of(d * TILE, TILE), TILE)
            dev = (((x + k) % X) * Z + (z + d) % Z, g)
            remote(p2.at[k, rows], emb.at[k, rows], s2_s.at[k], s2_r.at[k], dev).start()

        if k == 0:
            emb[0, :TILE, :] = p2[0, :TILE, :]

    slot_col = as_columns(slot.astype(F32)).astype(I32)
    for m in range(8):
        hot_t[:, m * 128 : (m + 1) * 128] = (
            (slot_col == iota((ROWS, 128), 1) + m * 128).astype(F32).astype(BF16)
        )
    perm_t[...] = (((i // 2) % 8) * PIECE + (i // TILE) * 2 + i % 2 == o).astype(F32).astype(BF16)
    live_col = as_columns(live.astype(F32)) == 1.0
    e_keep[...] = jnp.where(live_col, 0.25, 1.0) * e_keep[...]

    w2_group.wait_recv()
    w2_rows = jnp.concatenate(
        [w2_in[k // Z, k % Z] for k in range(64)] + [jnp.zeros((64, 128), F32)], axis=0
    ).astype(BF16)
    s, lane = iota((SLOTS, 128), 0), iota((SLOTS, 128), 1)
    spread = dot((s // TILE == lane).astype(F32).astype(BF16), w2_rows)
    own = jnp.where(s % TILE == lane, spread, 0.0).astype(BF16)
    w_col = dot(own, jnp.ones((128, 128), BF16))
    rw = jnp.where(w_col > 0, 1.0 / jnp.where(w_col > 0, w_col, 1.0), 0.0)
    rw_col[...] = rw
    rw_row[...] = as_row(rw)

    for k in DX_ORDER:
        arrived = tiles(k, p2.at[k], emb.at[k], s2_s.at[k], s2_r.at[k])
        arrived.wait_recv()
        sent.append(arrived)

    rows = emb[...].reshape(SLOTS, COMPS)
    wide = rows.astype(F32)
    norm = jnp.broadcast_to(jnp.sum(wide * wide, axis=1, keepdims=True), (SLOTS, 128))
    norm_row = as_row(norm)
    present = (rw_col[...] > 0).astype(F32).astype(BF16)
    with_ones = jnp.concatenate([rows, present], axis=1)
    for k in range(4):
        part = slice(k * CHUNK, (k + 1) * CHUNK)
        products = dot_nt(rows[part], rows)
        distance = norm[part, 0:1] + norm_row - 2.0 * products
        affinity = jnp.exp(-distance * rw_col[part, 0:1] * rw_row[...]).astype(BF16)
        aff[k] = affinity
        both = dot(affinity, with_ones)
        here = rw_col[part, :] > 0
        inverse = jnp.where(here, 1.0 / jnp.where(here, both[:, COMPS:], 1.0), 0.0)
        moved = both[:, :COMPS] * inverse
        o_keep[k] = 0.25 * moved
        rw_col[part, :] = 0.5 * inverse
        s1_ref[part, :] = jnp.where(here, 0.5 * (wide[part] + moved), 0.0).astype(BF16)

    for k in DX_ORDER:
        part = slice(k * CHUNK, (k + 1) * CHUNK)
        p3[k] = (o_keep[k] + rw_col[part, :] * dot(aff[k], s1_ref[...])).astype(BF16)

        @pl.loop(0, Z - 1 if k == 0 else Z)
        def _(t):
            d = far_first(t)
            rows = pl.ds(pl.multiple_of(d * TILE, TILE), TILE)
            dev = (((x - k + X) % X) * Z + (z - d + Z) % Z, g)
            remote(p3.at[k, rows], r3.at[k, rows], s3_s.at[k], s3_r.at[k], dev).start()

        if k == 0:
            r3[0, :TILE, :] = p3[0, :TILE, :]

    for k in DX_ORDER:
        arrived = tiles(k, p3.at[k], r3.at[k], s3_s.at[k], s3_r.at[k])
        arrived.wait_recv()
        sent.append(arrived)
        p4[k] = dot(perm_t[...], r3[k]).astype(BF16)

        @pl.loop(1, GROUP)
        def _(d):
            to = (g + d) % GROUP
            remote(
                p4.at[k, pl.ds(pl.multiple_of(to * PIECE, PIECE), PIECE)],
                r4.at[k, pl.ds(pl.multiple_of(g * PIECE, PIECE), PIECE)],
                s4_s.at[k], s4_r.at[k], (q, to),
            ).start()

        mine = pl.ds(pl.multiple_of(g * PIECE, PIECE), PIECE)
        r4[k, mine, :] = p4[k, mine, :]

    total = e_keep[...]
    for k in DX_ORDER:
        arrived = all_but_one(p4.at[k], r4.at[k], s4_s.at[k], s4_r.at[k])
        arrived.wait_recv()
        sent.append(arrived)
        total += dot(hot_t[:, k * CHUNK : (k + 1) * CHUNK], r4[k])
    out_ref[...] = total

    finish()


def body(expression, loading, kernel_width, cluster, quality):
    hbm = pl.BlockSpec(memory_space=pltpu.HBM)
    vmem = pl.BlockSpec(memory_space=pltpu.VMEM)
    dma = pltpu.SemaphoreType.DMA
    chunks = pltpu.VMEM((4, CHUNK, COMPS), BF16)
    operands = [
        pltpu.with_memory_space_constraint(a, pltpu.HBM)
        for a in (
            expression,
            loading,
            kernel_width,
            cluster.reshape(1, ROWS),
            quality.reshape(1, ROWS),
        )
    ]
    return pl.pallas_call(
        kernel,
        out_shape=jax.ShapeDtypeStruct((ROWS, COMPS), F32),
        in_specs=[hbm] * 5,
        out_specs=vmem,
        scratch_shapes=[
            pltpu.VMEM((8, ROWS, 512), BF16),
            pltpu.VMEM((4, ROWS, COMPS), F32),
            pltpu.VMEM((CHUNK, CHUNK), BF16),
            pltpu.VMEM((512, COMPS), BF16),
            pltpu.VMEM((ROWS,), BF16),
            pltpu.VMEM((1, ROWS), I32),
            pltpu.VMEM((1, ROWS), I32),
            pltpu.VMEM((4, ROWS, COMPS), F32),
            pltpu.VMEM((4, ROWS, COMPS), F32),
            pltpu.VMEM((ROWS, COMPS), BF16),
            pltpu.VMEM((2, HALF, COMPS), BF16),
            pltpu.VMEM((2, ROWS, COMPS), BF16),
            pltpu.VMEM((2, ROWS, COMPS), BF16),
            pltpu.VMEM((2, HALF, COMPS), F32),
            pltpu.VMEM((ROWS, COMPS), F32),
            pltpu.VMEM((SLOTS, ROWS), BF16),
            pltpu.VMEM((ROWS, SLOTS), BF16),
            chunks,
            chunks,
            chunks,
            chunks,
            pltpu.VMEM((GROUP, 1, 128), F32),
            pltpu.VMEM((GROUP, 1, 128), F32),
            pltpu.VMEM((X, Z, 1, 128), F32),
            pltpu.VMEM((X, Z, 1, 128), F32),
            pltpu.VMEM((X, Z, 1, 128), F32),
            pltpu.VMEM((SLOTS, 128), F32),
            pltpu.VMEM((1, SLOTS), F32),
            pltpu.VMEM((4, CHUNK, SLOTS), BF16),
            pltpu.VMEM((4, CHUNK, COMPS), F32),
            pltpu.VMEM((SLOTS, COMPS), BF16),
            chunks,
            chunks,
            chunks,
            chunks,
            dma((8,)), dma((4,)), dma((4,)), dma((4,)), dma((2,)), dma((2,)), dma((4,)), dma((4,)),
            dma((4,)), dma((4,)), dma((4,)), dma((4,)), dma((4,)), dma((4,)), dma((4,)), dma((4,)),
            dma, dma, dma((4,)), dma((4,)), dma, dma,
        ],
        compiler_params=pltpu.CompilerParams(
            collective_id=0, has_side_effects=True, vmem_limit_bytes=48 * 1024 * 1024
        ),
    )(*operands)


def solution(mesh):
    return jax.shard_map(
        body,
        mesh=mesh,
        in_specs=(
            P("cells", "genes"),
            P("genes", None),
            P(("cells", "genes")),
            P(("cells", "genes"), None),
            P(("cells", "genes")),
        ),
        out_specs=P(("cells", "genes"), None),
        check_vma=False,
    )
```

```python
import functools

import jax
import jax.numpy as jnp
from jax import lax
from jax.experimental import pallas as pl
from jax.experimental.pallas import tpu as pltpu
from jax.sharding import PartitionSpec as P

MESH = pl.DeviceIdType.MESH
F32 = jnp.float32
BF16 = jnp.bfloat16
I32 = jnp.int32

X, Z, Y = 4, 16, 4
GROUP = 8
ROWS = 512
HALF = ROWS // 2
COMPS = 128
SLOTS = 1024
CHUNK = 256
PIECE = 32
TILE = 16
DY_ORDER = (2, 1, 3, 0)
OUT_ORDER = (0, 1, 3, 2)
BACK_ORDER = (2, 1, 3, 0)


def iota(shape, dim):
    return lax.broadcasted_iota(I32, shape, dim)


def dot(a, b):
    return jnp.dot(a, b, preferred_element_type=F32)


def dot_nt(a, b):
    return lax.dot_general(a, b, (((1,), (1,)), ((), ())), preferred_element_type=F32)


def as_columns(row):
    n = row.shape[1]
    return jnp.concatenate(
        [jnp.broadcast_to(row[:, m : m + 128], (128, 128)).T for m in range(0, n, 128)], axis=0
    )


def as_row(columns):
    n = columns.shape[0]
    return jnp.concatenate([columns[m : m + 128, :].T[0:1, :] for m in range(0, n, 128)], axis=1)


def far_first(t):
    return 8 + (1 - 2 * (t % 2)) * ((t + 1) // 2)


def near(d):
    return 4 + (2 * (d % 2) - 1) * (d // 2) + 4 * (1 - (d + 7) // 8)


def kernel(
    expr, load_hbm, width_hbm, cluster_hbm, quality_hbm, out_ref,
    xbuf, parts, perm_t, load_ref, width_ref, cluster_ref, quality_ref, sib_out, sib_in, a_out, a_in, b_out, b_in, s_keep, e_keep,
    hot, hot_t, p1, r1, p2, emb, w1, w1_in, w2, wx, wz, w2_in, rw_col, rw_row,
    aff, norm_col, norm_row, ones, both, o_keep, s1_ref, p3, rz, p4, r4,
    x_sem, in_sem, sib_s, sib_r, a_s, a_r, b_s, b_r, s1_s, s1_r, s2_s, s2_r, s3_s, s3_r, s4_s, s4_r,
    w1_s, w1_r, wx_s, wx_r, w2_s, w2_r,
):
    q = lax.axis_index("cells")
    g = lax.axis_index("genes")
    x, z = q // Z, q % Z
    y, core = g // 2, g % 2
    other = 1 - core

    def remote(src, dst, ssem, rsem, dev):
        return pltpu.make_async_remote_copy(
            src_ref=src, dst_ref=dst, send_sem=ssem, recv_sem=rsem,
            device_id=dev, device_id_type=MESH,
        )

    def at_y(dy):
        return (q, ((y + dy) % Y) * 2 + core)

    sibling = (q, y * 2 + other)
    sent = []

    def finish():
        for copy in sent:
            copy.wait_send()

    def fetch(i):
        dy, c = DY_ORDER[i % 4], (other if i < 4 else core)
        block = ((y + dy) % Y) * 2 + c
        return pltpu.make_async_copy(
            expr.at[pl.ds(pl.multiple_of(block * ROWS, ROWS), ROWS)], xbuf.at[i], x_sem.at[i]
        )

    small = [
        pltpu.make_async_copy(src, dst, in_sem.at[i])
        for i, (src, dst) in enumerate(
            [
                (load_hbm, load_ref),
                (cluster_hbm, cluster_ref),
                (quality_hbm, quality_ref),
                (width_hbm, width_ref),
            ]
        )
    ]
    small[0].start()
    for i in range(4):
        fetch(i).start()
        fetch(4 + i).start()
    for copy in small[1:]:
        copy.start()

    barrier = pltpu.get_barrier_semaphore()

    def along_z(d):
        return (x * Z + (z + d + Z) % Z, g)

    def in_plane(k, to):
        return (((x + k + X) % X) * Z + z, to)

    @pl.loop(0, Z - 1)
    def _(t):
        pl.semaphore_signal(barrier, 1, device_id=along_z(far_first(t)), device_id_type=MESH)

    @pl.loop(1, X * GROUP)
    def _(n):
        dev = in_plane(n // GROUP, (g + n) % GROUP)
        pl.semaphore_signal(barrier, 1, device_id=dev, device_id_type=MESH)

    small[0].wait()
    loading = load_ref[...]
    sib_copies = [
        remote(sib_out.at[i], sib_in.at[i], sib_s.at[i], sib_r.at[i], sibling) for i in range(4)
    ]
    sent.extend(sib_copies)

    def for_sibling(i):
        fetch(i).wait()
        sib_out[i] = dot(xbuf[i], loading).astype(BF16)

    def for_own(i):
        fetch(4 + i).wait()
        parts[i] = dot(xbuf[4 + i], loading)

    def chip_sum(i):
        sib_copies[i].wait_recv()
        return parts[i] + sib_in[i].astype(F32)

    for_sibling(0)
    pl.semaphore_wait(barrier, Z - 1 + X * GROUP - 1)
    sib_copies[0].start()
    for_own(0)
    for_sibling(1)
    sib_copies[1].start()

    up, down = at_y(1), at_y(3)
    low, high = pl.ds(0, HALF), pl.ds(HALF, HALF)
    a_out[...] = chip_sum(0).astype(BF16)
    a_up = remote(a_out.at[low], a_in.at[0], a_s.at[0], a_r.at[0], up)
    a_down = remote(a_out.at[high], a_in.at[1], a_s.at[1], a_r.at[1], down)
    a_up.start()
    sent.append(a_up)
    a_down.start()
    sent.append(a_down)
    for_own(1)
    for_sibling(2)
    sib_copies[2].start()
    part = chip_sum(1)
    b_out[0, HALF:, :] = part[HALF:].astype(BF16)
    b_up_high = remote(b_out.at[0, high], b_in.at[0, high], b_s.at[0], b_r.at[0], up)
    b_up_high.start()
    sent.append(b_up_high)
    s_keep[0] = part[:HALF]
    for_own(2)
    for_sibling(3)
    sib_copies[3].start()
    part = chip_sum(2)
    b_out[1, :HALF, :] = part[:HALF].astype(BF16)
    b_down_low = remote(b_out.at[1, low], b_in.at[1, low], b_s.at[1], b_r.at[1], down)
    b_down_low.start()
    sent.append(b_down_low)
    s_keep[1] = part[HALF:]
    for_own(3)

    for copy in small[1:]:
        copy.wait()
    cluster = cluster_ref[...]
    live = quality_ref[...] == 1
    owner = cluster % (X * Z)
    gd = cluster // (X * Z)
    dx = (owner // Z - x + X) % X
    dz = (owner % Z - z + Z) % Z
    key = jnp.where(live, cluster, -1).astype(F32)
    key_col = as_columns(key)
    ranks = []
    for m in range(4):
        row = key[:, m * 128 : m * 128 + 128]
        same = (key_col[m * 128 : m * 128 + 128] == row) & (
            iota((128, 128), 0) < iota((128, 128), 1)
        )
        rank = jnp.sum(same.astype(F32), axis=0, keepdims=True)
        for k in range(m):
            same = key_col[k * 128 : k * 128 + 128] == row
            rank += jnp.sum(same.astype(F32), axis=0, keepdims=True)
        ranks.append(rank)
    rank = jnp.concatenate(ranks, axis=1).astype(I32)
    slot = jnp.where(live, dx * CHUNK + gd * PIECE + dz * 2 + rank, -1)
    place = jnp.where(live, dx * PIECE + dz * 2 + rank, -1)
    a_up.wait_recv()
    b_out[0, :HALF, :] = (s_keep[0] + a_in[0].astype(F32)).astype(BF16)
    b_up_low = remote(b_out.at[0, low], b_in.at[0, low], b_s.at[2], b_r.at[2], up)
    b_up_low.start()
    sent.append(b_up_low)
    a_down.wait_recv()
    b_out[1, HALF:, :] = (s_keep[1] + a_in[1].astype(F32)).astype(BF16)
    b_down_high = remote(b_out.at[1, high], b_in.at[1, high], b_s.at[3], b_r.at[3], down)
    b_down_high.start()
    sent.append(b_down_high)

    width = width_ref[...].reshape(1, ROWS).astype(F32)
    m1 = jnp.where((iota((16, ROWS), 0) == gd) & live, width, 0.0).astype(BF16)
    m2 = (as_columns(place.astype(F32)).astype(I32) == iota((ROWS, 128), 1)).astype(F32).astype(BF16)
    w1_all = dot(m1, m2)
    for k in range(GROUP):
        w1[k] = w1_all[k : k + 1]
    w1_in[g] = w1[g]

    @pl.loop(1, GROUP)
    def _(d):
        to = (g + near(d)) % GROUP
        remote(w1.at[to], w1_in.at[g], w1_s, w1_r, (q, to)).start()

    for m in range(4):
        hot[m * CHUNK : (m + 1) * CHUNK, :] = (
            (iota((CHUNK, ROWS), 0) + m * CHUNK == slot).astype(F32).astype(BF16)
        )
    w1_group = remote(w1.at[pl.ds(0, 7)], w1_in.at[pl.ds(0, 7)], w1_s, w1_r, sibling)
    sent.append(w1_group)
    o, i = iota((CHUNK, CHUNK), 0), iota((CHUNK, CHUNK), 1)
    perm = (((o // 2) % 8) * PIECE + (o // TILE) * 2 + o % 2 == i).astype(F32).astype(BF16)

    b_up_high.wait_recv()
    b_down_low.wait_recv()
    b_up_low.wait_recv()
    b_down_high.wait_recv()
    embedded = chip_sum(3) + b_in[0].astype(F32) + b_in[1].astype(F32)
    e_keep[...] = embedded
    e_rows = embedded.astype(BF16)

    def scatter_plane(k, src, dst, ssem, rsem, sign):
        @pl.loop(0 if k else 1, GROUP)
        def _(d):
            to = (g + near(d)) % GROUP
            remote(
                src.at[k, pl.ds(pl.multiple_of(to * PIECE, PIECE), PIECE)],
                dst.at[k, pl.ds(pl.multiple_of(g * PIECE, PIECE), PIECE)],
                ssem.at[k], rsem.at[k], in_plane(sign * k, to),
            ).start()

        if k == 0:
            mine = pl.ds(pl.multiple_of(g * PIECE, PIECE), PIECE)
            dst[0, mine, :] = src[0, mine, :]

    def pieces(k, src, dst, ssem, rsem):
        n = CHUNK if k else CHUNK - PIECE
        return remote(
            src.at[k, pl.ds(0, n)], dst.at[k, pl.ds(0, n)], ssem.at[k], rsem.at[k], sibling
        )

    def scatter_z(k, src, dst, ssem, rsem, sign):
        @pl.loop(0, Z - 1)
        def _(t):
            d = far_first(t)
            rows = pl.ds(pl.multiple_of(d * TILE, TILE), TILE)
            remote(
                src.at[k, rows], dst.at[k, rows], ssem.at[k], rsem.at[k], along_z(sign * d)
            ).start()

        dst[k, :TILE, :] = src[k, :TILE, :]

    def tiles(k, src, dst, ssem, rsem):
        n = CHUNK - TILE
        return remote(
            src.at[k, pl.ds(0, n)], dst.at[k, pl.ds(0, n)], ssem.at[k], rsem.at[k], sibling
        )

    for k in OUT_ORDER:
        p1[k] = dot(hot[k * CHUNK : (k + 1) * CHUNK, :], e_rows).astype(BF16)
        scatter_plane(k, p1, r1, s1_s, s1_r, 1)

    w1_group.wait_recv()
    w1_rows = jnp.concatenate(
        [w1_in[k] for k in range(GROUP)] + [jnp.zeros((120, 128), F32)], axis=0
    ).astype(BF16)
    w2_all = jnp.zeros((64, 128), F32)
    for r in range(2):
        pick = (iota((64, 128), 0) * 2 + r == iota((64, 128), 1)).astype(F32).astype(BF16)
        put = (iota((128, 128), 0) * 2 + r == iota((128, 128), 1) % TILE).astype(F32).astype(BF16)
        w2_all += dot(dot_nt(pick, w1_rows).astype(BF16), put)
    w2_all = jnp.where(iota((64, 128), 0) // Z == iota((64, 128), 1) // TILE, w2_all, 0.0)
    for k in range(64):
        w2[k // Z, k % Z] = w2_all[k : k + 1]
    for k in range(Z):
        wx[0, k] = w2[0, k]
    for k in range(1, X):
        sent.append(
            remote(w2.at[k], wx.at[k], wx_s.at[k], wx_r.at[k], (((x + k) % X) * Z + z, g))
        )
        sent[-1].start()
    wx_copies = sent[-3:]

    def widths_along_z():
        for copy in wx_copies:
            copy.wait_recv()
        for k in range(Z):
            wz[k] = wx[0, k] + wx[1, k] + wx[2, k] + wx[3, k]
        w2_in[0] = wz[0]

        @pl.loop(0, Z - 1)
        def _(t):
            d = far_first(t)
            remote(wz.at[d], w2_in.at[d], w2_s, w2_r, (x * Z + (z + d) % Z, g)).start()

    w2_group = remote(wz.at[pl.ds(0, Z - 1)], w2_in.at[pl.ds(0, Z - 1)], w2_s, w2_r, sibling)
    sent.append(w2_group)

    for k in OUT_ORDER:
        arrived = pieces(k, p1, r1, s1_s, s1_r)
        arrived.wait_recv()
        sent.append(arrived)
        p2[k] = dot(perm, r1[k]).astype(BF16)
        if k == OUT_ORDER[2]:
            widths_along_z()
        scatter_z(k, p2, emb, s2_s, s2_r, 1)

    slot_col = as_columns(slot.astype(F32)).astype(I32)
    for m in range(8):
        hot_t[:, m * 128 : (m + 1) * 128] = (
            (slot_col == iota((ROWS, 128), 1) + m * 128).astype(F32).astype(BF16)
        )
    perm_t[...] = (((i // 2) % 8) * PIECE + (i // TILE) * 2 + i % 2 == o).astype(F32).astype(BF16)
    live_col = as_columns(live.astype(F32)) == 1.0
    e_keep[...] = jnp.where(live_col, 0.25, 1.0) * e_keep[...]

    w2_group.wait_recv()
    w2_rows = jnp.concatenate(
        [w2_in[k] for k in range(Z)] + [jnp.zeros((128 - Z, 128), F32)], axis=0
    ).astype(BF16)
    s, lane = iota((SLOTS, 128), 0), iota((SLOTS, 128), 1)
    spread = dot((s // TILE % Z == lane).astype(F32).astype(BF16), w2_rows)
    own = jnp.where(s // CHUNK * TILE + s % TILE == lane, spread, 0.0).astype(BF16)
    w_col = dot(own, jnp.ones((128, 128), BF16))
    rw = jnp.where(w_col > 0, 1.0 / jnp.where(w_col > 0, w_col, 1.0), 0.0)
    rw_col[...] = rw
    rw_row[...] = as_row(rw)

    begun = set()
    for n, k in enumerate(OUT_ORDER):
        arrived = tiles(k, p2, emb, s2_s, s2_r)
        arrived.wait_recv()
        sent.append(arrived)
        part = slice(k * CHUNK, (k + 1) * CHUNK)
        wide = emb[k].astype(F32)
        norm = jnp.broadcast_to(jnp.sum(wide * wide, axis=1, keepdims=True), (CHUNK, 128))
        norm_col[k] = norm
        norm_row[:, part] = as_row(norm)
        ones[k] = jnp.concatenate(
            [emb[k], (rw_col[part, :] > 0).astype(F32).astype(BF16)], axis=1
        )
        seen = OUT_ORDER[: n + 1]
        for a, b in [(k, m) for m in seen] + [(m, k) for m in seen[:-1]]:
            at_a, at_b = slice(a * CHUNK, (a + 1) * CHUNK), slice(b * CHUNK, (b + 1) * CHUNK)
            distance = (
                norm_col[a][:, 0:1] + norm_row[:, at_b] - 2.0 * dot_nt(emb[a], emb[b])
            )
            affinity = jnp.exp(-distance * rw_col[at_a, 0:1] * rw_row[:, at_b]).astype(BF16)
            aff[a, :, at_b] = affinity
            moved = dot(affinity, ones[b])
            both[a] = both[a] + moved if a in begun else moved
            begun.add(a)
    for k in range(4):
        part = slice(k * CHUNK, (k + 1) * CHUNK)
        here = rw_col[part, :] > 0
        inverse = jnp.where(here, 1.0 / jnp.where(here, both[k, :, COMPS:], 1.0), 0.0)
        moved = both[k, :, :COMPS] * inverse
        o_keep[k] = 0.25 * moved
        rw_col[part, :] = 0.5 * inverse
        s1_ref[part, :] = jnp.where(here, 0.5 * (emb[k].astype(F32) + moved), 0.0).astype(BF16)

    for k in BACK_ORDER:
        part = slice(k * CHUNK, (k + 1) * CHUNK)
        p3[k] = (o_keep[k] + rw_col[part, :] * dot(aff[k], s1_ref[...])).astype(BF16)
        scatter_z(k, p3, rz, s3_s, s3_r, -1)

    for k in BACK_ORDER:
        arrived = tiles(k, p3, rz, s3_s, s3_r)
        arrived.wait_recv()
        sent.append(arrived)
        p4[k] = dot(perm_t[...], rz[k]).astype(BF16)
        scatter_plane(k, p4, r4, s4_s, s4_r, -1)

    total = e_keep[...]
    for k in BACK_ORDER:
        arrived = pieces(k, p4, r4, s4_s, s4_r)
        arrived.wait_recv()
        sent.append(arrived)
        total += dot(hot_t[:, k * CHUNK : (k + 1) * CHUNK], r4[k])
    out_ref[...] = total

    finish()


def body(expression, loading, kernel_width, cluster, quality):
    hbm = pl.BlockSpec(memory_space=pltpu.HBM)
    vmem = pl.BlockSpec(memory_space=pltpu.VMEM)
    dma = pltpu.SemaphoreType.DMA
    chunks = pltpu.VMEM((4, CHUNK, COMPS), BF16)
    operands = [
        pltpu.with_memory_space_constraint(a, pltpu.HBM)
        for a in (
            expression,
            loading,
            kernel_width,
            cluster.reshape(1, ROWS),
            quality.reshape(1, ROWS),
        )
    ]
    return pl.pallas_call(
        kernel,
        out_shape=jax.ShapeDtypeStruct((ROWS, COMPS), F32),
        in_specs=[hbm] * 5,
        out_specs=vmem,
        scratch_shapes=[
            pltpu.VMEM((8, ROWS, 512), BF16),
            pltpu.VMEM((4, ROWS, COMPS), F32),
            pltpu.VMEM((CHUNK, CHUNK), BF16),
            pltpu.VMEM((512, COMPS), BF16),
            pltpu.VMEM((ROWS,), BF16),
            pltpu.VMEM((1, ROWS), I32),
            pltpu.VMEM((1, ROWS), I32),
            pltpu.VMEM((4, ROWS, COMPS), BF16),
            pltpu.VMEM((4, ROWS, COMPS), BF16),
            pltpu.VMEM((ROWS, COMPS), BF16),
            pltpu.VMEM((2, HALF, COMPS), BF16),
            pltpu.VMEM((2, ROWS, COMPS), BF16),
            pltpu.VMEM((2, ROWS, COMPS), BF16),
            pltpu.VMEM((2, HALF, COMPS), F32),
            pltpu.VMEM((ROWS, COMPS), F32),
            pltpu.VMEM((SLOTS, ROWS), BF16),
            pltpu.VMEM((ROWS, SLOTS), BF16),
            chunks,
            chunks,
            chunks,
            chunks,
            pltpu.VMEM((GROUP, 1, 128), F32),
            pltpu.VMEM((GROUP, 1, 128), F32),
            pltpu.VMEM((X, Z, 1, 128), F32),
            pltpu.VMEM((X, Z, 1, 128), F32),
            pltpu.VMEM((Z, 1, 128), F32),
            pltpu.VMEM((Z, 1, 128), F32),
            pltpu.VMEM((SLOTS, 128), F32),
            pltpu.VMEM((1, SLOTS), F32),
            pltpu.VMEM((4, CHUNK, SLOTS), BF16),
            pltpu.VMEM((4, CHUNK, 128), F32),
            pltpu.VMEM((1, SLOTS), F32),
            pltpu.VMEM((4, CHUNK, 2 * COMPS), BF16),
            pltpu.VMEM((4, CHUNK, 2 * COMPS), F32),
            pltpu.VMEM((4, CHUNK, COMPS), F32),
            pltpu.VMEM((SLOTS, COMPS), BF16),
            chunks,
            chunks,
            chunks,
            chunks,
            dma((8,)), dma((4,)), dma((4,)), dma((4,)), dma((2,)), dma((2,)), dma((4,)), dma((4,)),
            dma((4,)), dma((4,)), dma((4,)), dma((4,)), dma((4,)), dma((4,)), dma((4,)), dma((4,)),
            dma, dma, dma((4,)), dma((4,)), dma, dma,
        ],
        compiler_params=pltpu.CompilerParams(
            collective_id=0, has_side_effects=True, vmem_limit_bytes=48 * 1024 * 1024
        ),
    )(*operands)


def solution(mesh):
    return jax.shard_map(
        body,
        mesh=mesh,
        in_specs=(
            P("cells", "genes"),
            P("genes", None),
            P(("cells", "genes")),
            P(("cells", "genes"), None),
            P(("cells", "genes")),
        ),
        out_specs=P(("cells", "genes"), None),
        check_vma=False,
    )
```

```python
import functools

import jax
import jax.numpy as jnp
from jax import lax
from jax.experimental import pallas as pl
from jax.experimental.pallas import tpu as pltpu
from jax.sharding import PartitionSpec as P

MESH = pl.DeviceIdType.MESH
F32 = jnp.float32
BF16 = jnp.bfloat16
I32 = jnp.int32

X, Z, Y = 4, 16, 4
GROUP = 8
ROWS = 512
HALF = ROWS // 2
COMPS = 128
SLOTS = 1024
CHUNK = 256
PIECE = 32
TILE = 16
DY_ORDER = (2, 1, 3, 0)
OUT_ORDER = (0, 1, 3, 2)
BACK_ORDER = (2, 1, 3, 0)


def iota(shape, dim):
    return lax.broadcasted_iota(I32, shape, dim)


def dot(a, b):
    return jnp.dot(a, b, preferred_element_type=F32)


def dot_nt(a, b):
    return lax.dot_general(a, b, (((1,), (1,)), ((), ())), preferred_element_type=F32)


def as_columns(row):
    n = row.shape[1]
    return jnp.concatenate(
        [jnp.broadcast_to(row[:, m : m + 128], (128, 128)).T for m in range(0, n, 128)], axis=0
    )


def as_row(columns):
    n = columns.shape[0]
    return jnp.concatenate([columns[m : m + 128, :].T[0:1, :] for m in range(0, n, 128)], axis=1)


def far_first(t):
    return 8 + (1 - 2 * (t % 2)) * ((t + 1) // 2)


def near(d):
    return 4 + (2 * (d % 2) - 1) * (d // 2) + 4 * (1 - (d + 7) // 8)


def kernel(
    expr, load_hbm, width_hbm, cluster_hbm, quality_hbm, out_ref,
    xbuf, parts, perm_t, load_ref, width_ref, cluster_ref, quality_ref, sib_out, sib_in, a_out, a_in, b_out, b_in, s_keep, e_keep,
    hot, hot_t, p1, r1, p2, emb, w1, w1_in, w2, wx, wz, w2_in, rw_col, rw_row,
    aff, norm_col, norm_row, ones, both, o_keep, s1_ref, p3, rz, p4, r4,
    x_sem, in_sem, sib_s, sib_r, a_s, a_r, b_s, b_r, s1_s, s1_r, s2_s, s2_r, s3_s, s3_r, s4_s, s4_r,
    w1_s, w1_r, wx_s, wx_r, w2_s, w2_r,
):
    q = lax.axis_index("cells")
    g = lax.axis_index("genes")
    x, z = q // Z, q % Z
    y, core = g // 2, g % 2
    other = 1 - core

    def remote(src, dst, ssem, rsem, dev):
        return pltpu.make_async_remote_copy(
            src_ref=src, dst_ref=dst, send_sem=ssem, recv_sem=rsem,
            device_id=dev, device_id_type=MESH,
        )

    def at_y(dy):
        return (q, ((y + dy) % Y) * 2 + core)

    sibling = (q, y * 2 + other)
    sent = []

    def finish():
        for copy in sent:
            copy.wait_send()

    def fetch(i):
        dy, c = DY_ORDER[i % 4], (other if i < 4 else core)
        block = ((y + dy) % Y) * 2 + c
        return pltpu.make_async_copy(
            expr.at[pl.ds(pl.multiple_of(block * ROWS, ROWS), ROWS)], xbuf.at[i], x_sem.at[i]
        )

    small = [
        pltpu.make_async_copy(src, dst, in_sem.at[i])
        for i, (src, dst) in enumerate(
            [
                (load_hbm, load_ref),
                (cluster_hbm, cluster_ref),
                (quality_hbm, quality_ref),
                (width_hbm, width_ref),
            ]
        )
    ]
    small[0].start()
    for i in range(4):
        fetch(i).start()
        fetch(4 + i).start()
    for copy in small[1:]:
        copy.start()

    barrier = pltpu.get_barrier_semaphore()

    def along_z(d):
        return (x * Z + (z + d + Z) % Z, g)

    def in_plane(k, to):
        return (((x + k + X) % X) * Z + z, to)

    @pl.loop(0, Z - 1)
    def _(t):
        pl.semaphore_signal(barrier, 1, device_id=along_z(far_first(t)), device_id_type=MESH)

    @pl.loop(1, X * GROUP)
    def _(n):
        dev = in_plane(n // GROUP, (g + n) % GROUP)
        pl.semaphore_signal(barrier, 1, device_id=dev, device_id_type=MESH)

    small[0].wait()
    loading = load_ref[...]
    sib_copies = [
        remote(sib_out.at[i], sib_in.at[i], sib_s.at[i], sib_r.at[i], sibling) for i in range(4)
    ]
    sent.extend(sib_copies)

    def for_sibling(i):
        fetch(i).wait()
        sib_out[i] = dot(xbuf[i], loading).astype(BF16)

    def for_own(i):
        fetch(4 + i).wait()
        parts[i] = dot(xbuf[4 + i], loading)

    def chip_sum(i):
        sib_copies[i].wait_recv()
        return parts[i] + sib_in[i].astype(F32)

    for_sibling(0)
    pl.semaphore_wait(barrier, Z - 1 + X * GROUP - 1)
    sib_copies[0].start()
    for_own(0)
    for_sibling(1)
    sib_copies[1].start()

    up, down = at_y(1), at_y(3)
    low, high = pl.ds(0, HALF), pl.ds(HALF, HALF)
    a_out[...] = chip_sum(0).astype(BF16)
    a_up = remote(a_out.at[low], a_in.at[0], a_s.at[0], a_r.at[0], up)
    a_down = remote(a_out.at[high], a_in.at[1], a_s.at[1], a_r.at[1], down)
    a_up.start()
    sent.append(a_up)
    a_down.start()
    sent.append(a_down)
    for_own(1)
    for_sibling(2)
    sib_copies[2].start()
    part = chip_sum(1)
    b_out[0, HALF:, :] = part[HALF:].astype(BF16)
    b_up_high = remote(b_out.at[0, high], b_in.at[0, high], b_s.at[0], b_r.at[0], up)
    b_up_high.start()
    sent.append(b_up_high)
    s_keep[0] = part[:HALF]
    for_own(2)
    for_sibling(3)
    sib_copies[3].start()
    part = chip_sum(2)
    b_out[1, :HALF, :] = part[:HALF].astype(BF16)
    b_down_low = remote(b_out.at[1, low], b_in.at[1, low], b_s.at[1], b_r.at[1], down)
    b_down_low.start()
    sent.append(b_down_low)
    s_keep[1] = part[HALF:]
    for_own(3)

    for copy in small[1:]:
        copy.wait()
    cluster = cluster_ref[...]
    live = quality_ref[...] == 1
    owner = cluster % (X * Z)
    gd = cluster // (X * Z)
    dx = (owner // Z - x + X) % X
    dz = (owner % Z - z + Z) % Z
    key = jnp.where(live, cluster, -1).astype(F32)
    key_col = as_columns(key)
    ranks = []
    for m in range(4):
        row = key[:, m * 128 : m * 128 + 128]
        same = (key_col[m * 128 : m * 128 + 128] == row) & (
            iota((128, 128), 0) < iota((128, 128), 1)
        )
        rank = jnp.sum(same.astype(F32), axis=0, keepdims=True)
        for k in range(m):
            same = key_col[k * 128 : k * 128 + 128] == row
            rank += jnp.sum(same.astype(F32), axis=0, keepdims=True)
        ranks.append(rank)
    rank = jnp.concatenate(ranks, axis=1).astype(I32)
    slot = jnp.where(live, dx * CHUNK + gd * PIECE + dz * 2 + rank, -1)
    place = jnp.where(live, dx * PIECE + dz * 2 + rank, -1)
    a_up.wait_recv()
    b_out[0, :HALF, :] = (s_keep[0] + a_in[0].astype(F32)).astype(BF16)
    b_up_low = remote(b_out.at[0, low], b_in.at[0, low], b_s.at[2], b_r.at[2], up)
    b_up_low.start()
    sent.append(b_up_low)
    a_down.wait_recv()
    b_out[1, HALF:, :] = (s_keep[1] + a_in[1].astype(F32)).astype(BF16)
    b_down_high = remote(b_out.at[1, high], b_in.at[1, high], b_s.at[3], b_r.at[3], down)
    b_down_high.start()
    sent.append(b_down_high)

    width = width_ref[...].reshape(1, ROWS).astype(F32)
    m1 = jnp.where((iota((16, ROWS), 0) == gd) & live, width, 0.0).astype(BF16)
    m2 = (as_columns(place.astype(F32)).astype(I32) == iota((ROWS, 128), 1)).astype(F32).astype(BF16)
    w1_all = dot(m1, m2)
    for k in range(GROUP):
        w1[k] = w1_all[k : k + 1]
    w1_in[g] = w1[g]

    @pl.loop(1, GROUP)
    def _(d):
        to = (g + near(d)) % GROUP
        remote(w1.at[to], w1_in.at[g], w1_s, w1_r, (q, to)).start()

    for m in range(4):
        hot[m * CHUNK : (m + 1) * CHUNK, :] = (
            (iota((CHUNK, ROWS), 0) + m * CHUNK == slot).astype(F32).astype(BF16)
        )
    w1_group = remote(w1.at[pl.ds(0, 7)], w1_in.at[pl.ds(0, 7)], w1_s, w1_r, sibling)
    sent.append(w1_group)
    o, i = iota((CHUNK, CHUNK), 0), iota((CHUNK, CHUNK), 1)
    perm = (((o // 2) % 8) * PIECE + (o // TILE) * 2 + o % 2 == i).astype(F32).astype(BF16)

    b_up_high.wait_recv()
    b_down_low.wait_recv()
    b_up_low.wait_recv()
    b_down_high.wait_recv()
    embedded = chip_sum(3) + b_in[0].astype(F32) + b_in[1].astype(F32)
    e_keep[...] = embedded
    e_rows = embedded.astype(BF16)

    def scatter_plane(k, src, dst, ssem, rsem, sign):
        @pl.loop(0 if k else 1, GROUP)
        def _(d):
            to = (g + near(d)) % GROUP
            remote(
                src.at[k, pl.ds(pl.multiple_of(to * PIECE, PIECE), PIECE)],
                dst.at[k, pl.ds(pl.multiple_of(g * PIECE, PIECE), PIECE)],
                ssem.at[k], rsem.at[k], in_plane(sign * k, to),
            ).start()

        if k == 0:
            mine = pl.ds(pl.multiple_of(g * PIECE, PIECE), PIECE)
            dst[0, mine, :] = src[0, mine, :]

    def pieces(k, src, dst, ssem, rsem):
        n = CHUNK if k else CHUNK - PIECE
        return remote(
            src.at[k, pl.ds(0, n)], dst.at[k, pl.ds(0, n)], ssem.at[k], rsem.at[k], sibling
        )

    def scatter_z(k, src, dst, ssem, rsem, sign):
        @pl.loop(0, Z - 1)
        def _(t):
            d = far_first(t)
            rows = pl.ds(pl.multiple_of(d * TILE, TILE), TILE)
            remote(
                src.at[k, rows], dst.at[k, rows], ssem.at[k], rsem.at[k], along_z(sign * d)
            ).start()

        dst[k, :TILE, :] = src[k, :TILE, :]

    def tiles(k, src, dst, ssem, rsem):
        n = CHUNK - TILE
        return remote(
            src.at[k, pl.ds(0, n)], dst.at[k, pl.ds(0, n)], ssem.at[k], rsem.at[k], sibling
        )

    for k in OUT_ORDER:
        p1[k] = dot(hot[k * CHUNK : (k + 1) * CHUNK, :], e_rows).astype(BF16)
        scatter_plane(k, p1, r1, s1_s, s1_r, 1)

    w1_group.wait_recv()
    w1_rows = jnp.concatenate(
        [w1_in[k] for k in range(GROUP)] + [jnp.zeros((120, 128), F32)], axis=0
    ).astype(BF16)
    w2_all = jnp.zeros((64, 128), F32)
    for r in range(2):
        pick = (iota((64, 128), 0) * 2 + r == iota((64, 128), 1)).astype(F32).astype(BF16)
        put = (iota((128, 128), 0) * 2 + r == iota((128, 128), 1) % TILE).astype(F32).astype(BF16)
        w2_all += dot(dot_nt(pick, w1_rows).astype(BF16), put)
    w2_all = jnp.where(iota((64, 128), 0) // Z == iota((64, 128), 1) // TILE, w2_all, 0.0)
    for k in range(64):
        w2[k // Z, k % Z] = w2_all[k : k + 1]
    for k in range(Z):
        wx[0, k] = w2[0, k]
    for k in range(1, X):
        sent.append(
            remote(w2.at[k], wx.at[k], wx_s.at[k], wx_r.at[k], (((x + k) % X) * Z + z, g))
        )
        sent[-1].start()
    wx_copies = sent[-3:]

    def widths_along_z():
        for copy in wx_copies:
            copy.wait_recv()
        for k in range(Z):
            wz[k] = wx[0, k] + wx[1, k] + wx[2, k] + wx[3, k]
        w2_in[0] = wz[0]

        @pl.loop(0, Z - 1)
        def _(t):
            d = far_first(t)
            remote(wz.at[d], w2_in.at[d], w2_s, w2_r, (x * Z + (z + d) % Z, g)).start()

    w2_group = remote(wz.at[pl.ds(0, Z - 1)], w2_in.at[pl.ds(0, Z - 1)], w2_s, w2_r, sibling)
    sent.append(w2_group)

    for k in OUT_ORDER:
        arrived = pieces(k, p1, r1, s1_s, s1_r)
        arrived.wait_recv()
        sent.append(arrived)
        p2[k] = dot(perm, r1[k]).astype(BF16)
        if k == OUT_ORDER[2]:
            widths_along_z()
        scatter_z(k, p2, emb, s2_s, s2_r, 1)

    slot_col = as_columns(slot.astype(F32)).astype(I32)
    for m in range(8):
        hot_t[:, m * 128 : (m + 1) * 128] = (
            (slot_col == iota((ROWS, 128), 1) + m * 128).astype(F32).astype(BF16)
        )
    perm_t[...] = (((i // 2) % 8) * PIECE + (i // TILE) * 2 + i % 2 == o).astype(F32).astype(BF16)
    live_col = as_columns(live.astype(F32)) == 1.0
    e_keep[...] = jnp.where(live_col, 0.25, 1.0) * e_keep[...]

    w2_group.wait_recv()
    w2_rows = jnp.concatenate(
        [w2_in[k] for k in range(Z)] + [jnp.zeros((128 - Z, 128), F32)], axis=0
    ).astype(BF16)
    s, lane = iota((SLOTS, 128), 0), iota((SLOTS, 128), 1)
    spread = dot((s // TILE % Z == lane).astype(F32).astype(BF16), w2_rows)
    own = jnp.where(s // CHUNK * TILE + s % TILE == lane, spread, 0.0).astype(BF16)
    w_col = dot(own, jnp.ones((128, 128), BF16))
    rw = jnp.where(w_col > 0, 1.0 / jnp.where(w_col > 0, w_col, 1.0), 0.0)
    rw_col[...] = rw
    rw_row[...] = as_row(rw)

    begun = set()
    for n, k in enumerate(OUT_ORDER):
        arrived = tiles(k, p2, emb, s2_s, s2_r)
        arrived.wait_recv()
        sent.append(arrived)
        part = slice(k * CHUNK, (k + 1) * CHUNK)
        wide = emb[k].astype(F32)
        norm = jnp.broadcast_to(jnp.sum(wide * wide, axis=1, keepdims=True), (CHUNK, 128))
        norm_col[k] = norm
        norm_row[:, part] = as_row(norm)
        ones[k] = jnp.concatenate(
            [emb[k], (rw_col[part, :] > 0).astype(F32).astype(BF16)], axis=1
        )
        seen = OUT_ORDER[: n + 1]
        for a, b in [(k, m) for m in seen] + [(m, k) for m in seen[:-1]]:
            at_a, at_b = slice(a * CHUNK, (a + 1) * CHUNK), slice(b * CHUNK, (b + 1) * CHUNK)
            distance = (
                norm_col[a][:, 0:1] + norm_row[:, at_b] - 2.0 * dot_nt(emb[a], emb[b])
            )
            affinity = jnp.exp(-distance * rw_col[at_a, 0:1] * rw_row[:, at_b]).astype(BF16)
            aff[a, :, at_b] = affinity
            moved = dot(affinity, ones[b])
            both[a] = both[a] + moved if a in begun else moved
            begun.add(a)
    for k in range(4):
        part = slice(k * CHUNK, (k + 1) * CHUNK)
        here = rw_col[part, :] > 0
        inverse = jnp.where(here, 1.0 / jnp.where(here, both[k, :, COMPS:], 1.0), 0.0)
        moved = both[k, :, :COMPS] * inverse
        o_keep[k] = 0.25 * moved
        rw_col[part, :] = 0.5 * inverse
        s1_ref[part, :] = jnp.where(here, 0.5 * (emb[k].astype(F32) + moved), 0.0).astype(BF16)

    for k in BACK_ORDER:
        part = slice(k * CHUNK, (k + 1) * CHUNK)
        p3[k] = (o_keep[k] + rw_col[part, :] * dot(aff[k], s1_ref[...])).astype(BF16)
        scatter_z(k, p3, rz, s3_s, s3_r, -1)

    finish()
    sent.clear()

    for k in BACK_ORDER:
        arrived = tiles(k, p3, rz, s3_s, s3_r)
        arrived.wait_recv()
        sent.append(arrived)
        p4[k] = dot(perm_t[...], rz[k]).astype(BF16)
        scatter_plane(k, p4, r4, s4_s, s4_r, -1)

    total = e_keep[...]
    for k in BACK_ORDER:
        arrived = pieces(k, p4, r4, s4_s, s4_r)
        arrived.wait_recv()
        sent.append(arrived)
        total += dot(hot_t[:, k * CHUNK : (k + 1) * CHUNK], r4[k])
    out_ref[...] = total

    finish()


def body(expression, loading, kernel_width, cluster, quality):
    hbm = pl.BlockSpec(memory_space=pltpu.HBM)
    vmem = pl.BlockSpec(memory_space=pltpu.VMEM)
    dma = pltpu.SemaphoreType.DMA
    chunks = pltpu.VMEM((4, CHUNK, COMPS), BF16)
    operands = [
        pltpu.with_memory_space_constraint(a, pltpu.HBM)
        for a in (
            expression,
            loading,
            kernel_width,
            cluster.reshape(1, ROWS),
            quality.reshape(1, ROWS),
        )
    ]
    return pl.pallas_call(
        kernel,
        out_shape=jax.ShapeDtypeStruct((ROWS, COMPS), F32),
        in_specs=[hbm] * 5,
        out_specs=vmem,
        scratch_shapes=[
            pltpu.VMEM((8, ROWS, 512), BF16),
            pltpu.VMEM((4, ROWS, COMPS), F32),
            pltpu.VMEM((CHUNK, CHUNK), BF16),
            pltpu.VMEM((512, COMPS), BF16),
            pltpu.VMEM((ROWS,), BF16),
            pltpu.VMEM((1, ROWS), I32),
            pltpu.VMEM((1, ROWS), I32),
            pltpu.VMEM((4, ROWS, COMPS), BF16),
            pltpu.VMEM((4, ROWS, COMPS), BF16),
            pltpu.VMEM((ROWS, COMPS), BF16),
            pltpu.VMEM((2, HALF, COMPS), BF16),
            pltpu.VMEM((2, ROWS, COMPS), BF16),
            pltpu.VMEM((2, ROWS, COMPS), BF16),
            pltpu.VMEM((2, HALF, COMPS), F32),
            pltpu.VMEM((ROWS, COMPS), F32),
            pltpu.VMEM((SLOTS, ROWS), BF16),
            pltpu.VMEM((ROWS, SLOTS), BF16),
            chunks,
            chunks,
            chunks,
            chunks,
            pltpu.VMEM((GROUP, 1, 128), F32),
            pltpu.VMEM((GROUP, 1, 128), F32),
            pltpu.VMEM((X, Z, 1, 128), F32),
            pltpu.VMEM((X, Z, 1, 128), F32),
            pltpu.VMEM((Z, 1, 128), F32),
            pltpu.VMEM((Z, 1, 128), F32),
            pltpu.VMEM((SLOTS, 128), F32),
            pltpu.VMEM((1, SLOTS), F32),
            pltpu.VMEM((4, CHUNK, SLOTS), BF16),
            pltpu.VMEM((4, CHUNK, 128), F32),
            pltpu.VMEM((1, SLOTS), F32),
            pltpu.VMEM((4, CHUNK, 2 * COMPS), BF16),
            pltpu.VMEM((4, CHUNK, 2 * COMPS), F32),
            pltpu.VMEM((4, CHUNK, COMPS), F32),
            pltpu.VMEM((SLOTS, COMPS), BF16),
            chunks,
            chunks,
            chunks,
            chunks,
            dma((8,)), dma((4,)), dma((4,)), dma((4,)), dma((2,)), dma((2,)), dma((4,)), dma((4,)),
            dma((4,)), dma((4,)), dma((4,)), dma((4,)), dma((4,)), dma((4,)), dma((4,)), dma((4,)),
            dma, dma, dma((4,)), dma((4,)), dma, dma,
        ],
        compiler_params=pltpu.CompilerParams(
            collective_id=0, has_side_effects=True, vmem_limit_bytes=48 * 1024 * 1024
        ),
    )(*operands)


def solution(mesh):
    return jax.shard_map(
        body,
        mesh=mesh,
        in_specs=(
            P("cells", "genes"),
            P("genes", None),
            P(("cells", "genes")),
            P(("cells", "genes"), None),
            P(("cells", "genes")),
        ),
        out_specs=P(("cells", "genes"), None),
        check_vma=False,
    )
```
